32 devices in a mesh: groups: 2 (over y), tensor: 4 (over z), dp: 2 (over x), pipe: 2 (over core).
Axes of the slice: x: 2, y: 2, z: 4, core: 2. Of those that a mesh axis runs over, the one named last changes fastest.
Arguments:
- activations: bfloat16 [4096, 8192], P(('groups', 'dp', 'pipe'), 'tensor'), parts along dimension 0, may hold values from -6 to 6
- query_weight: bfloat16 [8192, 8192], P(('dp', 'pipe'), 'tensor'), may hold values from -0.0625 to 0.0625
- offsets: int32 [66], P('groups'), parts along dimension 0, may hold values from 0 to 2048, as said below
- request_adapter: int32 [64], P('groups'), parts along dimension 0, may hold values from 0 to 1999, as said below
- page_table: int32 [4000], P('groups'), parts along dimension 0, may hold values from -1 to 63, as said below
- shrink_pages: bfloat16 [128, 8192, 64], P(('groups', 'dp', 'pipe'), 'tensor'), parts along dimension 0, may hold values from -0.0625 to 0.0625
- expand_pages: bfloat16 [128, 64, 8192], P(('groups', 'dp', 'pipe'), None, 'tensor'), parts along dimension 0, may hold values from -0.75 to 0.75
Outputs:
- queries: bfloat16 [4096, 8192], P(('groups', 'dp', 'pipe'), 'tensor'), parts along dimension 0
The draws below stay inside these ranges and needn't reach their ends.
There are 2 independent parts, one for each index of `groups`. The reference program is written for one: setup_inputs(seed, part) draws one part's arguments, and reference() takes and returns one part's arrays. A program takes and returns all parts, laid end to end along the dimension named above; an argument that names none is the same for every part. Nothing has to cross between parts.
Inputs may be any that keep to these rules, and one draw needn't show every extreme that they name: `offsets`: rises from 0 to 2048; every request holds 32 tokens or more, so the rows of one device meet at most 17 requests, and in every draw the rows of some device meet exactly 17. `request_adapter`: the requests use different resident adapters; request r sits on a page of the page shard (r + c) mod (number of devices along dp and pipe) for a constant c of the draw, so the rows of one device use at most 5 pages of any one shard, a bound that some device reaches in every draw. `page_table`: exactly 64 adapters are resident, each on its own page.
All inputs are finite; a program needn't handle non-finite values.
Results may differ from the reference program's by a relative error of at most 0.0065.
Values may be sent and summed in bfloat16 or wider, within the bound.
A program may use at most 192 MiB of HBM per device.

```python
import jax
import jax.numpy as jnp

D = 8192
R = 64
PAGES = 64
ADAPTERS = 2000
REQS = 32
TOK_DEV = 512
TOKENS = 2048
SHORTEST = 32
USED = 17
N_DP = 2
N_PIPE = 2


def resident_layout(key):
    order = jax.random.permutation(key, ADAPTERS).astype(jnp.int32)
    rotation = jax.random.randint(jax.random.fold_in(key, 11), (), 0, PAGES - REQS + 1).astype(jnp.int32)
    return (order, rotation)


def split_parts(key, count, extra):
    index = jnp.arange(REQS, dtype=jnp.int32)
    cuts = jax.random.randint(key, (REQS,), 0, extra + 1).astype(jnp.int32)
    cuts = jnp.where(index < count - 1, cuts, extra)
    cuts = jnp.sort(cuts)
    edges = jnp.concatenate([jnp.zeros((1,), jnp.int32), cuts])
    return (edges[1:] - edges[:-1]).astype(jnp.int32)


def draw_offsets(key, part):
    key = jax.random.fold_in(key, 3)
    shards = N_DP * N_PIPE
    short = SHORTEST
    most = USED
    key_block, key_head, key_tail = jax.random.split(key, 3)
    block = jax.random.randint(key_block, (), 1, shards - 1).astype(jnp.int32)
    head_count = jnp.maximum(1, block * (REQS - most + 1) // shards).astype(jnp.int32)
    head_total = block * TOK_DEV + 1
    tail_start = head_total + (most - 2) * short
    tail_count = REQS - head_count - (most - 2)
    tail_total = TOKENS - tail_start
    head = split_parts(key_head, head_count, head_total - head_count * short) + short
    tail = split_parts(key_tail, tail_count, tail_total - tail_count * short) + short
    index = jnp.arange(REQS, dtype=jnp.int32)
    tail_index = jnp.clip(index - head_count - (most - 2), 0, REQS - 1)
    lengths = jnp.where(index < head_count, head, jnp.where(index < head_count + most - 2, short, tail[tail_index]))
    return jnp.concatenate([jnp.zeros((1,), jnp.int32), jnp.cumsum(lengths).astype(jnp.int32)])


def draw_page_table(key, part):
    order, rotation = resident_layout(key)
    position = jnp.argsort(order, stable=True).astype(jnp.int32)
    return jnp.where(position < PAGES, position, -1).astype(jnp.int32)


def draw_request_adapter(key, part):
    order, rotation = resident_layout(key)
    shards = N_DP * N_PIPE
    per_shard = PAGES // shards
    spot = jnp.arange(REQS, dtype=jnp.int32) + rotation
    page = spot % shards * per_shard + spot // shards
    return order[page].astype(jnp.int32)


def block_levels(key, dims, cuts, low, high):
    gain = 1.0
    for dim, shards_of in cuts:
        steps = jax.random.uniform(jax.random.fold_in(jax.random.fold_in(key, 6), dim), (shards_of,), jnp.float32, low / len(cuts), high / len(cuts))
        gain = gain * jnp.repeat(jnp.exp(steps), dims[dim] // shards_of).reshape((-1,) + (1,) * (len(dims) - 1 - dim))
    return gain


def scatter_about(rng, extent, scale, bound, cuts=(), kind=jnp.bfloat16):
    values = jax.random.normal(rng, extent, jnp.float32) * scale
    if len(cuts) > 0:
        values = block_levels(rng, extent, cuts, -0.22, 0.18) * values
    return jnp.clip(values, min=-bound, max=bound).astype(kind)


def setup_inputs(seed: int = 0, part: int = 0) -> dict:
    key_of = jax.random.split(jax.random.key(seed), 8)
    own_keys = jax.random.split(jax.random.fold_in(key_of[7], part), 8)
    activations = scatter_about(own_keys[0], (TOKENS, D), 1.0, 6.0, ((0, 4), (1, 4)))
    query_weight = scatter_about(key_of[1], (D, D), D ** -0.5, 0.0625, ((0, 4), (1, 4)))
    offsets = draw_offsets(jax.random.fold_in(jax.random.fold_in(key_of[7], part), 71), part)
    request_adapter = draw_request_adapter(jax.random.fold_in(jax.random.fold_in(key_of[7], part), 71), part)
    page_table = draw_page_table(jax.random.fold_in(jax.random.fold_in(key_of[7], part), 71), part)
    shrink_pages = scatter_about(own_keys[5], (PAGES, D, R), D ** -0.5, 0.0625, ((0, 4), (1, 4)))
    expand_pages = scatter_about(own_keys[6], (PAGES, R, D), R ** -0.5, 0.75, ((0, 4), (2, 4)))
    return {"activations": activations, "query_weight": query_weight, "offsets": offsets, "request_adapter": request_adapter, "page_table": page_table, "shrink_pages": shrink_pages, "expand_pages": expand_pages}


def page_select(positions, offsets, request_adapter, page_table, count):
    adapter_ids = jnp.arange(page_table.shape[0], dtype=jnp.int32)
    match = (request_adapter[:, None] == adapter_ids[None, :]).astype(jnp.int32)
    page_of_request = jnp.sum(match * page_table[None, :], axis=1)
    inside = (offsets[None, :-1] <= positions[:, None]) & (positions[:, None] < offsets[None, 1:])
    page_of_token = jnp.sum(inside.astype(jnp.int32) * page_of_request[None, :], axis=1)
    slots = jnp.arange(count, dtype=jnp.int32)
    return (page_of_token[:, None] == slots[None, :]).astype(jnp.float32)


def reference(activations, query_weight, offsets, request_adapter, page_table, shrink_pages, expand_pages):
    positions = jnp.arange(activations.shape[0], dtype=jnp.int32)
    select = page_select(positions, offsets, request_adapter, page_table, shrink_pages.shape[0])
    base = jnp.dot(activations, query_weight, preferred_element_type=jnp.float32)
    scores = jnp.einsum("td,pdr->tpr", activations.astype(jnp.float32), shrink_pages.astype(jnp.float32))
    shrunk = jnp.sum(select[:, :, None] * scores, axis=1).astype(jnp.bfloat16)
    spread = (select[:, :, None] * shrunk[:, None, :].astype(jnp.float32)).astype(jnp.bfloat16)
    added = jnp.einsum("tpr,prc->tc", spread.astype(jnp.float32), expand_pages.astype(jnp.float32))
    return (base + added).astype(jnp.bfloat16)
```

```python
import jax
import jax.numpy as jnp
from jax import lax
from jax.experimental import pallas as pl
from jax.experimental.pallas import tpu as pltpu
from jax.sharding import PartitionSpec as P


def slot_table(offsets, request_adapter, page_table, first, rows, used):
    reqs = offsets.shape[0] - 1
    adapter_ids = jnp.arange(page_table.shape[0], dtype=jnp.int32)
    match = (request_adapter[:, None] == adapter_ids[None, :]).astype(jnp.int32)
    page_of_request = jnp.sum(match * page_table[None, :], axis=1)
    leading = jnp.sum((offsets[1:] <= first).astype(jnp.int32))
    wanted = leading + jnp.arange(used, dtype=jnp.int32)
    clipped = jnp.clip(wanted, 0, reqs - 1)
    valid = (wanted < reqs) & (offsets[clipped] < first + rows)
    return (leading, page_of_request[clipped], valid)


def token_select(positions, offsets, leading, used):
    request = jnp.sum((offsets[None, 1:] <= positions[:, None]).astype(jnp.int32), axis=1)
    slot_of = request - leading
    return (slot_of[:, None] == jnp.arange(used, dtype=jnp.int32)[None, :]).astype(jnp.float32)


def shrink_term(local, factors, select):
    scores = jnp.einsum("tf,kfr->tkr", local, factors, preferred_element_type=jnp.float32)
    return jnp.sum(select[:, :, None] * scores, axis=1)


def expand_term(shrunk, factors, select):
    spread = (select[:, :, None] * shrunk[:, None, :].astype(jnp.float32)).astype(jnp.bfloat16)
    return jnp.einsum("tkr,krc->tc", spread, factors, preferred_element_type=jnp.float32)


def body(
    activations, query_weight, offsets, request_adapter, page_table, shrink_pages, expand_pages
):
    rows = activations.shape[0]
    shards = lax.axis_size(("dp", "pipe"))
    reqs = offsets.shape[0] - 1
    shortest = rows * shards // (2 * reqs)
    used = (rows - 2) // shortest + 2
    here = lax.axis_index(("dp", "pipe"))
    first = here * rows
    positions = first + jnp.arange(rows, dtype=jnp.int32)
    leading, pages, valid = slot_table(offsets, request_adapter, page_table, first, rows, used)
    select = token_select(positions, offsets, leading, used)
    whole = lax.all_gather(activations, "tensor", axis=1, tiled=True)
    base = jnp.dot(
        whole,
        lax.all_gather(query_weight, ("dp", "pipe"), axis=0, tiled=True),
        preferred_element_type=jnp.float32,
    )
    shrink_all, expand_all = (
        lax.all_gather(shrink_pages, ("dp", "pipe"), axis=0, tiled=True),
        lax.all_gather(expand_pages, ("dp", "pipe"), axis=0, tiled=True),
    )
    shrink_used = jnp.take(shrink_all, pages, axis=0)
    expand_used = jnp.take(expand_all, pages, axis=0)
    partial_value = shrink_term(activations, shrink_used, select)
    shrunk = lax.psum(partial_value, "tensor").astype(jnp.bfloat16)
    added = expand_term(shrunk, expand_used, select)
    return (base + added).astype(jnp.bfloat16)


MESH = pl.DeviceIdType.MESH
LANES = 128
CHUNKS = 4
HALVES = 2


def relay_kernel(
    act, weight, shrink, expand, slots, out,
    xp, ab, wv, sv, ev, mv, part, rsb, sh, spread, cs, rc, sx, rx, ov,
    load_sem, own_send, own_recv, fwd_send, fwd_recv, xown_send, xown_recv,
    up_send, dn_send, flow_recv, rs_send, rs_recv, ag_send, ag_recv,
    cs_send, cs_recv, x_send, x_recv, out_sem,
):
    x, p, z = lax.axis_index("dp"), lax.axis_index("pipe"), lax.axis_index("tensor")
    nz = lax.axis_size("tensor")
    rows = act.shape[0]
    ch = rows // CHUNKS
    hf = rows // HALVES
    d = 2 * x + p
    core, other = {"pipe": 1 - p}, {"dp": 1 - x}
    origin = z == d

    def blk(k):
        return 2 * (x if k < 2 else 1 - x) + (p if k % 2 == 0 else 1 - p)

    def rcopy(src, dst, ss, rs, dev):
        return pltpu.make_async_remote_copy(
            src_ref=src, dst_ref=dst, send_sem=ss, recv_sem=rs, device_id=dev, device_id_type=MESH
        )

    def cr(c):
        return pl.ds(c * ch, ch)

    def hr(h):
        return pl.ds(h * hf, hf)

    loads = [
        pltpu.make_async_copy(act, xp.at[d], load_sem.at[0]),
        pltpu.make_async_copy(shrink, sv, load_sem.at[1]),
        pltpu.make_async_copy(slots, mv, load_sem.at[2]),
        pltpu.make_async_copy(weight, wv, load_sem.at[3]),
        pltpu.make_async_copy(expand, ev, load_sem.at[4]),
    ]
    for cp in loads:
        cp.start()
    barrier = pltpu.get_barrier_semaphore()
    for j in range(1, nz):
        pl.semaphore_signal(barrier, inc=1, device_id={"tensor": lax.rem(z + j, nz)}, device_id_type=MESH)
    pl.semaphore_signal(barrier, inc=1, device_id=core, device_id_type=MESH)
    pl.semaphore_signal(barrier, inc=1, device_id=other, device_id_type=MESH)
    pl.semaphore_wait(barrier, nz + 1)
    loads[0].wait()

    def own_x(c):
        s = xp.at[d, cr(c)]
        return rcopy(s, s, xown_send.at[c], xown_recv.at[c], other)

    def own_core(c):
        s = xp.at[d, cr(c)]
        return rcopy(s, s, own_send.at[c], own_recv.at[c], core)

    def fwd(c):
        s = xp.at[blk(2), cr(c)]
        return rcopy(s, s, fwd_send.at[c], fwd_recv.at[c], core)

    def flow(k, c, src, step):
        b = blk(k)
        sem = up_send if step == 1 else dn_send
        return rcopy(
            src.at[b, cr(c)], ab.at[b, cr(c)], sem.at[k, c], flow_recv.at[k, c], {"tensor": z + step}
        )

    up = (z >= d) & (z < nz - 1)
    dn = (z <= d) & (z > 0)

    def send_flow(k, c, src):
        @pl.when(up)
        def _():
            flow(k, c, src, 1).start()

        @pl.when(dn)
        def _():
            flow(k, c, src, -1).start()

    def relay(k, c):
        @pl.when(jnp.logical_not(origin))
        def _():
            s = ab.at[blk(k), cr(c)]
            rcopy(s, s, up_send.at[k, c], flow_recv.at[k, c], core).wait_recv()
            send_flow(k, c, ab)

    for c in range(CHUNKS):
        own_x(c).start()
        own_core(c).start()

        @pl.when(origin)
        def _():
            send_flow(0, c, xp)

    for c in range(CHUNKS):
        own_core(c).wait_recv()

        @pl.when(origin)
        def _():
            send_flow(1, c, xp)

        own_x(c).wait_recv()
        fwd(c).start()

        @pl.when(origin)
        def _():
            send_flow(2, c, xp)

        if c > 0:
            relay(0, c - 1)
            relay(1, c - 1)
        fwd(c).wait_recv()

        @pl.when(origin)
        def _():
            send_flow(3, c, xp)

    relay(0, CHUNKS - 1)
    relay(1, CHUNKS - 1)

    loads[1].wait()
    loads[2].wait()
    groups = sv.shape[1] // LANES

    def shrink_step(i, _):
        b, r = i // HALVES, pl.ds(pl.multiple_of((i % HALVES) * hf, hf), hf)
        scores = jnp.dot(xp[b, r, :], sv[...], preferred_element_type=jnp.float32)
        m = mv[b, r, :]
        total = jnp.zeros((hf, LANES), jnp.float32)
        for g in range(groups):
            total += jnp.where(m == 2 * g, scores[:, g * LANES:(g + 1) * LANES], 0.0)
        part[b, r, :] = total.astype(jnp.bfloat16)
        return 0

    lax.fori_loop(0, nz * HALVES, shrink_step, 0)

    def rs_copy(j):
        to = lax.rem(z + j, nz)
        return rcopy(part.at[to], rsb.at[j - 1], rs_send.at[j - 1], rs_recv.at[j - 1], {"tensor": to})

    def ag_copy(j):
        to = lax.rem(z + j, nz)
        return rcopy(sh.at[z], sh.at[z], ag_send.at[j - 1], ag_recv.at[j - 1], {"tensor": to})

    for j in range(1, nz):
        rs_copy(j).start()

    for c in range(1):
        relay(2, c)
        relay(3, c)
    for j in range(1, nz):
        rs_copy(j).wait_recv()
    total = part[z].astype(jnp.float32)
    for j in range(1, nz):
        total += rsb[j - 1].astype(jnp.float32)
    sh[z] = total.astype(jnp.bfloat16)
    for j in range(1, nz):
        ag_copy(j).start()
    relay(2, 1)
    relay(3, 1)
    for j in range(1, nz):
        ag_copy(j).wait_recv()
    loads[3].wait()
    loads[4].wait()

    @pl.when(origin)
    def _():
        cp = pltpu.make_async_copy(xp, ab, load_sem.at[5])
        cp.start()
        cp.wait()

    tile = min(512, wv.shape[1])

    def compute(k, h, emit):
        b = blk(k)
        m = mv[b, hr(h), :]
        s = sh[b, hr(h), :]
        for g in range(groups):
            spread[:, g * LANES:(g + 1) * LANES] = jnp.where(m == 2 * g, s, jnp.zeros_like(s))

        def step(n, _):
            cols = pl.ds(pl.multiple_of(n * tile, tile), tile)
            value = jnp.dot(ab[b, hr(h), :], wv[:, cols], preferred_element_type=jnp.float32)
            value += jnp.dot(spread[...], ev[:, cols], preferred_element_type=jnp.float32)
            emit(value, cols)
            return 0

        lax.fori_loop(0, wv.shape[1] // tile, step, 0)

    def core_copy(i, h):
        return rcopy(cs.at[i, hr(h)], rc.at[i, hr(h)], cs_send.at[i, h], cs_recv.at[i, h], core)

    def x_copy(h):
        return rcopy(sx.at[hr(h)], rx.at[hr(h)], x_send.at[h], x_recv.at[h], other)

    def out_copy(h):
        return pltpu.make_async_copy(ov.at[hr(h)], out.at[hr(h)], out_sem.at[h])

    def to_core(i, k, h):
        def emit(value, cols):
            cs[i, hr(h), cols] = value.astype(jnp.bfloat16)

        compute(k, h, emit)
        core_copy(i, h).start()

    def to_x(h):
        core_copy(1, h).wait_recv()

        def emit(value, cols):
            sx[hr(h), cols] = (value + rc[1, hr(h), cols].astype(jnp.float32)).astype(jnp.bfloat16)

        compute(2, h, emit)
        x_copy(h).start()

    for h in range(HALVES):
        if h > 0:
            for c in range(2 * h, 2 * h + 2):
                relay(2, c)
                relay(3, c)
        to_core(1, 3, h)
        if h == 0:
            to_core(0, 1, 0)
        to_x(h)
        if h == 0:
            to_core(0, 1, 1)

    for h in range(HALVES):
        core_copy(0, h).wait_recv()

        x_copy(h).wait_recv()

        def emit(value, cols):
            value += rc[0, hr(h), cols].astype(jnp.float32) + rx[hr(h), cols].astype(jnp.float32)
            ov[hr(h), cols] = value.astype(jnp.bfloat16)

        compute(0, h, emit)
        out_copy(h).start()

    for h in range(HALVES):
        out_copy(h).wait()
        core_copy(0, h).wait_send()
        core_copy(1, h).wait_send()
        x_copy(h).wait_send()
    for j in range(1, nz):
        rs_copy(j).wait_send()
        ag_copy(j).wait_send()
    for c in range(CHUNKS):
        own_x(c).wait_send()
        own_core(c).wait_send()
        fwd(c).wait_send()
    for k in range(4):
        for c in range(CHUNKS):

            @pl.when(up)
            def _():
                flow(k, c, ab, 1).wait_send()

            @pl.when(dn)
            def _():
                flow(k, c, ab, -1).wait_send()


def relay_body(
    activations, query_weight, offsets, request_adapter, page_table, shrink_pages, expand_pages
):
    rows, feats = activations.shape
    cols = query_weight.shape[1]
    shards = lax.axis_size(("dp", "pipe"))
    reqs = offsets.shape[0] - 1
    held, _, rank = shrink_pages.shape
    mine = reqs // shards
    shard = lax.axis_index(("dp", "pipe"))
    adapter_ids = jnp.arange(page_table.shape[0], dtype=jnp.int32)
    match = (request_adapter[:, None] == adapter_ids[None, :]).astype(jnp.int32)
    page_of_request = jnp.sum(match * page_table[None, :], axis=1)
    lead = (shard - page_of_request[0] // held + shards) % shards
    pages = page_of_request.reshape(mine, shards)
    hot = (jnp.arange(shards, dtype=jnp.int32) == lead).astype(jnp.int32)
    pages = jnp.clip(jnp.sum(pages * hot[None, :], axis=1) - shard * held, 0, held - 1)
    positions = jnp.arange(rows * shards, dtype=jnp.int32)
    request = jnp.sum((offsets[None, 1:] <= positions[:, None]).astype(jnp.int32), axis=1)
    slot = jnp.where(request % shards == lead, request // shards, -8)
    upper = (jnp.arange(LANES, dtype=jnp.int32) >= rank).astype(jnp.int32)
    slots = (slot[:, None] - upper[None, :]).reshape(shards, rows, LANES)
    shrink = jnp.take(shrink_pages, pages, axis=0).transpose(1, 0, 2).reshape(feats, mine * rank)
    expand = jnp.take(expand_pages, pages, axis=0).reshape(mine * rank, cols)
    bf, dma = jnp.bfloat16, pltpu.SemaphoreType.DMA
    hf = rows // HALVES
    nz = lax.axis_size("tensor")
    return pl.pallas_call(
        relay_kernel,
        out_shape=jax.ShapeDtypeStruct((rows, cols), bf),
        in_specs=[pl.BlockSpec(memory_space=pl.ANY)] * 5,
        out_specs=pl.BlockSpec(memory_space=pl.ANY),
        scratch_shapes=[
            pltpu.VMEM((shards, rows, feats), bf),
            pltpu.VMEM((shards, rows, feats), bf),
            pltpu.VMEM(query_weight.shape, bf),
            pltpu.VMEM(shrink.shape, bf),
            pltpu.VMEM(expand.shape, bf),
            pltpu.VMEM(slots.shape, jnp.int32),
            pltpu.VMEM((shards, rows, LANES), bf),
            pltpu.VMEM((nz - 1, rows, LANES), bf),
            pltpu.VMEM((shards, rows, LANES), bf),
            pltpu.VMEM((hf, mine * rank), bf),
            pltpu.VMEM((2, rows, cols), bf),
            pltpu.VMEM((2, rows, cols), bf),
            pltpu.VMEM((rows, cols), bf),
            pltpu.VMEM((rows, cols), bf),
            pltpu.VMEM((rows, cols), bf),
            dma((6,)),
            dma((CHUNKS,)), dma((CHUNKS,)), dma((CHUNKS,)), dma((CHUNKS,)), dma((CHUNKS,)), dma((CHUNKS,)),
            dma((4, CHUNKS)), dma((4, CHUNKS)), dma((4, CHUNKS)),
            dma((nz - 1,)), dma((nz - 1,)), dma((nz - 1,)), dma((nz - 1,)),
            dma((2, HALVES)), dma((2, HALVES)), dma((HALVES,)), dma((HALVES,)), dma((HALVES,)),
        ],
        compiler_params=pltpu.CompilerParams(
            collective_id=0, has_side_effects=True, vmem_limit_bytes=60 * 1024 * 1024
        ),
        cost_estimate=pl.CostEstimate(
            flops=2 * shards * rows * feats * cols, bytes_accessed=2 * feats * cols, transcendentals=0
        ),
    )(activations, query_weight, shrink, expand, slots)


def solution(mesh):
    small = mesh.shape["dp"] == 2 and mesh.shape["pipe"] == 2 and mesh.shape["tensor"] == 4
    return jax.shard_map(
        relay_body if small else body,
        mesh=mesh,
        in_specs=(
            P(("groups", "dp", "pipe"), "tensor"),
            P(("dp", "pipe"), "tensor"),
            P("groups"),
            P("groups"),
            P("groups"),
            P(("groups", "dp", "pipe"), "tensor", None),
            P(("groups", "dp", "pipe"), None, "tensor"),
        ),
        out_specs=P(("groups", "dp", "pipe"), "tensor"),
        check_vma=False,
    )
```

```python
import jax
import jax.numpy as jnp
from jax import lax
from jax.experimental import pallas as pl
from jax.experimental.pallas import tpu as pltpu
from jax.sharding import PartitionSpec as P


def slot_table(offsets, request_adapter, page_table, first, rows, used):
    reqs = offsets.shape[0] - 1
    adapter_ids = jnp.arange(page_table.shape[0], dtype=jnp.int32)
    match = (request_adapter[:, None] == adapter_ids[None, :]).astype(jnp.int32)
    page_of_request = jnp.sum(match * page_table[None, :], axis=1)
    leading = jnp.sum((offsets[1:] <= first).astype(jnp.int32))
    wanted = leading + jnp.arange(used, dtype=jnp.int32)
    clipped = jnp.clip(wanted, 0, reqs - 1)
    valid = (wanted < reqs) & (offsets[clipped] < first + rows)
    return (leading, page_of_request[clipped], valid)


def token_select(positions, offsets, leading, used):
    request = jnp.sum((offsets[None, 1:] <= positions[:, None]).astype(jnp.int32), axis=1)
    slot_of = request - leading
    return (slot_of[:, None] == jnp.arange(used, dtype=jnp.int32)[None, :]).astype(jnp.float32)


def shrink_term(local, factors, select):
    scores = jnp.einsum("tf,kfr->tkr", local, factors, preferred_element_type=jnp.float32)
    return jnp.sum(select[:, :, None] * scores, axis=1)


def expand_term(shrunk, factors, select):
    spread = (select[:, :, None] * shrunk[:, None, :].astype(jnp.float32)).astype(jnp.bfloat16)
    return jnp.einsum("tkr,krc->tc", spread, factors, preferred_element_type=jnp.float32)


def body(
    activations, query_weight, offsets, request_adapter, page_table, shrink_pages, expand_pages
):
    rows = activations.shape[0]
    shards = lax.axis_size(("dp", "pipe"))
    reqs = offsets.shape[0] - 1
    shortest = rows * shards // (2 * reqs)
    used = (rows - 2) // shortest + 2
    here = lax.axis_index(("dp", "pipe"))
    first = here * rows
    positions = first + jnp.arange(rows, dtype=jnp.int32)
    leading, pages, valid = slot_table(offsets, request_adapter, page_table, first, rows, used)
    select = token_select(positions, offsets, leading, used)
    whole = lax.all_gather(activations, "tensor", axis=1, tiled=True)
    base = jnp.dot(
        whole,
        lax.all_gather(query_weight, ("dp", "pipe"), axis=0, tiled=True),
        preferred_element_type=jnp.float32,
    )
    shrink_all, expand_all = (
        lax.all_gather(shrink_pages, ("dp", "pipe"), axis=0, tiled=True),
        lax.all_gather(expand_pages, ("dp", "pipe"), axis=0, tiled=True),
    )
    shrink_used = jnp.take(shrink_all, pages, axis=0)
    expand_used = jnp.take(expand_all, pages, axis=0)
    partial_value = shrink_term(activations, shrink_used, select)
    shrunk = lax.psum(partial_value, "tensor").astype(jnp.bfloat16)
    added = expand_term(shrunk, expand_used, select)
    return (base + added).astype(jnp.bfloat16)


MESH = pl.DeviceIdType.MESH
LANES = 128
CHUNKS = 8
HALVES = 2


def relay_kernel(
    act, weight, shrink, expand, slots, out,
    xp, ab, fb, stage, wv, sv, ev, mv, part, rsb, sh, spread, cs, rc, sx, rx, ov,
    load_sem, own_send, own_recv, fwd_send, fwd_recv, xown_send, xown_recv,
    up_send, dn_send, flow_recv, f_send, f_recv, c_send, stage_sem, rs_send, rs_recv, ag_send, ag_recv,
    cs_send, cs_recv, x_send, x_recv, out_sem,
):
    x, p, z = lax.axis_index("dp"), lax.axis_index("pipe"), lax.axis_index("tensor")
    nz = lax.axis_size("tensor")
    rows = act.shape[0]
    ch = rows // CHUNKS
    hf = rows // HALVES
    d = 2 * x + p
    core, other = {"pipe": 1 - p}, {"dp": 1 - x}
    origin = z == d

    def blk(k):
        return 2 * (x if k < 2 else 1 - x) + (p if k % 2 == 0 else 1 - p)

    def rcopy(src, dst, ss, rs, dev):
        return pltpu.make_async_remote_copy(
            src_ref=src, dst_ref=dst, send_sem=ss, recv_sem=rs, device_id=dev, device_id_type=MESH
        )

    def cr(c):
        return pl.ds(c * ch, ch)

    def hr(h):
        return pl.ds(h * hf, hf)

    loads = [
        pltpu.make_async_copy(act, xp.at[d], load_sem.at[0]),
        pltpu.make_async_copy(slots, mv, load_sem.at[2]),
        pltpu.make_async_copy(weight, wv, load_sem.at[3]),
        pltpu.make_async_copy(expand, ev, load_sem.at[4]),
    ]
    for cp in loads:
        cp.start()
    barrier = pltpu.get_barrier_semaphore()
    for j in range(1, nz):
        pl.semaphore_signal(barrier, inc=1, device_id={"tensor": lax.rem(z + j, nz)}, device_id_type=MESH)
    pl.semaphore_signal(barrier, inc=1, device_id=core, device_id_type=MESH)
    pl.semaphore_signal(barrier, inc=1, device_id=other, device_id_type=MESH)
    pl.semaphore_wait(barrier, nz + 1)
    loads[0].wait()
    pairs = shrink.shape[0] // 2

    def stage_copy(i):
        return pltpu.make_async_copy(
            shrink.at[pl.ds(2 * i, 2)], stage.at[i % 2], stage_sem.at[i % 2]
        )

    stage_copy(0).start()
    stage_copy(1).start()

    def gather_pair(i):
        stage_copy(i).wait()
        sv[:, i * LANES:(i + 1) * LANES] = jnp.concatenate([stage[i % 2, 0], stage[i % 2, 1]], axis=1)
        if i + 2 < pairs:
            stage_copy(i + 2).start()

    def own_x(c):
        s = xp.at[d, cr(c)]
        return rcopy(s, s, xown_send.at[c], xown_recv.at[c], other)

    def own_core(c):
        s = xp.at[d, cr(c)]
        return rcopy(s, s, own_send.at[c], own_recv.at[c], core)

    def fwd(c):
        s = xp.at[blk(2), cr(c)]
        return rcopy(s, s, fwd_send.at[c], fwd_recv.at[c], core)

    def flow(k, c, src, step):
        b = blk(k)
        sem = up_send if step == 1 else dn_send
        return rcopy(
            src.at[b, cr(c)], ab.at[b, cr(c)], sem.at[k, c], flow_recv.at[k, c], {"tensor": z + step}
        )

    up = (z >= d) & (z < nz - 1)
    dn = (z <= d) & (z > 0)

    def goes(k, step):
        if k != 2:
            return up if step == 1 else dn
        return (up & (x == 1)) if step == 1 else (dn & (x == 0))

    def send_flow(k, c, src):
        @pl.when(goes(k, 1))
        def _():
            flow(k, c, src, 1).start()

        @pl.when(goes(k, -1))
        def _():
            flow(k, c, src, -1).start()

    def arrive(k, c):
        s = ab.at[blk(k), cr(c)]
        rcopy(s, s, up_send.at[k, c], flow_recv.at[k, c], core).wait_recv()

    def relay(k, c):
        @pl.when(jnp.logical_not(origin))
        def _():
            arrive(k, c)
            send_flow(k, c, ab)

    dx = blk(2)
    f_origin = z == dx
    f_member = ((x == 1) & (z > dx)) | ((x == 0) & (z < dx))
    f_next = (f_origin | f_member) & (((x == 1) & (z < nz - 1)) | ((x == 0) & (z > 0)))

    def f_copy(c, src):
        return rcopy(src, fb.at[cr(c)], f_send.at[c], f_recv.at[c], {"tensor": z + 2 * x - 1})

    def cross(c):
        return rcopy(fb.at[cr(c)], ab.at[d, cr(c)], c_send.at[c], flow_recv.at[2, c], other)

    def f_relay(c):
        @pl.when(f_member)
        def _():
            s = fb.at[cr(c)]
            rcopy(s, s, f_send.at[c], f_recv.at[c], core).wait_recv()

            @pl.when(f_next)
            def _():
                f_copy(c, fb.at[cr(c)]).start()

            cross(c).start()

    for c in range(CHUNKS):
        own_x(c).start()
        own_core(c).start()

        @pl.when(f_origin & f_next)
        def _():
            f_copy(c, xp.at[d, cr(c)]).start()

    def relays(c):
        relay(1, c)
        f_relay(c)
        relay(3, c)

    steps = CHUNKS // 2
    for i in range(steps):
        for c in (2 * i, 2 * i + 1):
            own_core(c).wait_recv()

            @pl.when(origin)
            def _():
                send_flow(1, c, xp)

            own_x(c).wait_recv()
            fwd(c).start()

            @pl.when(origin)
            def _():
                send_flow(2, c, xp)

            fwd(c).wait_recv()

            @pl.when(origin)
            def _():
                send_flow(3, c, xp)

        for g in range(i * pairs // steps, (i + 1) * pairs // steps):
            gather_pair(g)
        if i > 0:
            relays(i - 1)

    @pl.when(origin)
    def _():
        for c in range(CHUNKS):
            send_flow(0, c, xp)

    loads[1].wait()
    groups = sv.shape[1] // LANES

    def shrink_step(i, _):
        b, r = i // HALVES, pl.ds(pl.multiple_of((i % HALVES) * hf, hf), hf)
        scores = jnp.dot(xp[b, r, :], sv[...], preferred_element_type=jnp.float32)
        m = mv[b, r, :]
        total = jnp.zeros((hf, LANES), jnp.float32)
        for g in range(groups):
            total += jnp.where(m == 2 * g, scores[:, g * LANES:(g + 1) * LANES], 0.0)
        part[b, r, :] = total.astype(jnp.bfloat16)
        return 0

    lax.fori_loop(0, nz * HALVES, shrink_step, 0)

    def rs_copy(j):
        to = lax.rem(z + j, nz)
        return rcopy(part.at[to], rsb.at[j - 1], rs_send.at[j - 1], rs_recv.at[j - 1], {"tensor": to})

    def ag_copy(j):
        to = lax.rem(z + j, nz)
        return rcopy(sh.at[z], sh.at[z], ag_send.at[j - 1], ag_recv.at[j - 1], {"tensor": to})

    for j in range(1, nz):
        rs_copy(j).start()
    relays(3)
    relays(4)
    for j in range(1, nz):
        rs_copy(j).wait_recv()
    total = part[z].astype(jnp.float32)
    for j in range(1, nz):
        total += rsb[j - 1].astype(jnp.float32)
    sh[z] = total.astype(jnp.bfloat16)
    for j in range(1, nz):
        ag_copy(j).start()
    relays(5)
    for j in range(1, nz):
        ag_copy(j).wait_recv()
    loads[2].wait()
    loads[3].wait()

    @pl.when(origin)
    def _():
        cp = pltpu.make_async_copy(xp, ab, load_sem.at[5])
        cp.start()
        cp.wait()

    tile = min(512, wv.shape[1])

    def compute(k, h, emit):
        b = blk(k)
        m = mv[b, hr(h), :]
        s = sh[b, hr(h), :]
        for g in range(groups):
            spread[:, g * LANES:(g + 1) * LANES] = jnp.where(m == 2 * g, s, jnp.zeros_like(s))

        def step(n, _):
            cols = pl.ds(pl.multiple_of(n * tile, tile), tile)
            value = jnp.dot(ab[b, hr(h), :], wv[:, cols], preferred_element_type=jnp.float32)
            value += jnp.dot(spread[...], ev[:, :, cols].reshape(spread.shape[1], tile), preferred_element_type=jnp.float32)
            emit(value, cols)
            return 0

        lax.fori_loop(0, wv.shape[1] // tile, step, 0)

    def core_copy(i, h):
        return rcopy(cs.at[i, hr(h)], rc.at[i, hr(h)], cs_send.at[i, h], cs_recv.at[i, h], core)

    def x_copy(h):
        return rcopy(sx.at[hr(h)], rx.at[hr(h)], x_send.at[h], x_recv.at[h], other)

    def out_copy(h):
        return pltpu.make_async_copy(ov.at[hr(h)], out.at[hr(h)], out_sem.at[h])

    def to_core(i, k, h):
        def emit(value, cols):
            cs[i, hr(h), cols] = value.astype(jnp.bfloat16)

        compute(k, h, emit)
        core_copy(i, h).start()

    def to_x(h):
        core_copy(1, h).wait_recv()

        def emit(value, cols):
            sx[hr(h), cols] = (value + rc[1, hr(h), cols].astype(jnp.float32)).astype(jnp.bfloat16)

        compute(2, h, emit)
        x_copy(h).start()

    per = CHUNKS // HALVES

    def arrive_half(h):
        @pl.when(jnp.logical_not(origin))
        def _():
            for c in range(per * h, per * (h + 1)):
                arrive(2, c)

    to_core(1, 3, 0)
    relays(6)
    to_core(0, 1, 0)
    relays(7)
    to_core(1, 3, 1)
    relay(0, 0)
    relay(0, 1)
    arrive_half(0)
    to_x(0)
    relay(0, 2)
    relay(0, 3)
    to_core(0, 1, 1)
    relay(0, 4)
    arrive_half(1)
    to_x(1)
    for c in range(5, CHUNKS):
        relay(0, c)

    for h in range(HALVES):
        core_copy(0, h).wait_recv()

        x_copy(h).wait_recv()

        def emit(value, cols):
            value += rc[0, hr(h), cols].astype(jnp.float32) + rx[hr(h), cols].astype(jnp.float32)
            ov[hr(h), cols] = value.astype(jnp.bfloat16)

        compute(0, h, emit)
        out_copy(h).start()

    for h in range(HALVES):
        out_copy(h).wait()
        core_copy(0, h).wait_send()
        core_copy(1, h).wait_send()
        x_copy(h).wait_send()
    for j in range(1, nz):
        rs_copy(j).wait_send()
        ag_copy(j).wait_send()
    for c in range(CHUNKS):
        own_x(c).wait_send()
        own_core(c).wait_send()
        fwd(c).wait_send()
    for c in range(CHUNKS):
        for k in range(4):

            @pl.when(goes(k, 1))
            def _():
                flow(k, c, ab, 1).wait_send()

            @pl.when(goes(k, -1))
            def _():
                flow(k, c, ab, -1).wait_send()

        @pl.when(f_next)
        def _():
            f_copy(c, fb.at[cr(c)]).wait_send()

        @pl.when(f_member)
        def _():
            cross(c).wait_send()


def relay_body(
    activations, query_weight, offsets, request_adapter, page_table, shrink_pages, expand_pages
):
    rows, feats = activations.shape
    cols = query_weight.shape[1]
    shards = lax.axis_size(("dp", "pipe"))
    held, _, rank = shrink_pages.shape
    shard = lax.axis_index(("dp", "pipe"))
    adapter_ids = jnp.arange(page_table.shape[0], dtype=jnp.int32)
    match = (request_adapter[:, None] == adapter_ids[None, :]).astype(jnp.int32)
    page_of_request = jnp.sum(match * page_table[None, :], axis=1)
    positions = jnp.arange(rows * shards, dtype=jnp.int32)
    inside = (offsets[None, :-1] <= positions[:, None]) & (positions[:, None] < offsets[None, 1:])
    slot = jnp.sum(jnp.where(inside, page_of_request[None, :], 0), axis=1) - shard * held
    slot = jnp.where((slot >= 0) & (slot < held), slot, -8)
    upper = (jnp.arange(LANES, dtype=jnp.int32) >= rank).astype(jnp.int32)
    slots = (slot[:, None] - upper[None, :]).reshape(shards, rows, LANES)
    bf, dma = jnp.bfloat16, pltpu.SemaphoreType.DMA
    hf = rows // HALVES
    nz = lax.axis_size("tensor")
    return pl.pallas_call(
        relay_kernel,
        out_shape=jax.ShapeDtypeStruct((rows, cols), bf),
        in_specs=[pl.BlockSpec(memory_space=pl.ANY)] * 5,
        out_specs=pl.BlockSpec(memory_space=pl.ANY),
        scratch_shapes=[
            pltpu.VMEM((shards, rows, feats), bf),
            pltpu.VMEM((shards, rows, feats), bf),
            pltpu.VMEM((rows, feats), bf),
            pltpu.VMEM((2, 2, feats, rank), bf),
            pltpu.VMEM(query_weight.shape, bf),
            pltpu.VMEM((feats, held * rank), bf),
            pltpu.VMEM(expand_pages.shape, bf),
            pltpu.VMEM(slots.shape, jnp.int32),
            pltpu.VMEM((shards, rows, LANES), bf),
            pltpu.VMEM((nz - 1, rows, LANES), bf),
            pltpu.VMEM((shards, rows, LANES), bf),
            pltpu.VMEM((hf, held * rank), bf),
            pltpu.VMEM((2, rows, cols), bf),
            pltpu.VMEM((2, rows, cols), bf),
            pltpu.VMEM((rows, cols), bf),
            pltpu.VMEM((rows, cols), bf),
            pltpu.VMEM((rows, cols), bf),
            dma((6,)),
            dma((CHUNKS,)), dma((CHUNKS,)), dma((CHUNKS,)), dma((CHUNKS,)), dma((CHUNKS,)), dma((CHUNKS,)),
            dma((4, CHUNKS)), dma((4, CHUNKS)), dma((4, CHUNKS)),
            dma((CHUNKS,)), dma((CHUNKS,)), dma((CHUNKS,)), dma((2,)),
            dma((nz - 1,)), dma((nz - 1,)), dma((nz - 1,)), dma((nz - 1,)),
            dma((2, HALVES)), dma((2, HALVES)), dma((HALVES,)), dma((HALVES,)), dma((HALVES,)),
        ],
        compiler_params=pltpu.CompilerParams(
            collective_id=0, has_side_effects=True, vmem_limit_bytes=62 * 1024 * 1024
        ),
        cost_estimate=pl.CostEstimate(
            flops=2 * shards * rows * feats * cols, bytes_accessed=2 * feats * cols, transcendentals=0
        ),
    )(activations, query_weight, shrink_pages, expand_pages, slots)


def solution(mesh):
    small = mesh.shape["dp"] == 2 and mesh.shape["pipe"] == 2 and mesh.shape["tensor"] == 4
    return jax.shard_map(
        relay_body if small else body,
        mesh=mesh,
        in_specs=(
            P(("groups", "dp", "pipe"), "tensor"),
            P(("dp", "pipe"), "tensor"),
            P("groups"),
            P("groups"),
            P("groups"),
            P(("groups", "dp", "pipe"), "tensor", None),
            P(("groups", "dp", "pipe"), None, "tensor"),
        ),
        out_specs=P(("groups", "dp", "pipe"), "tensor"),
        check_vma=False,
    )
```

```python
import jax
import jax.numpy as jnp
from jax import lax
from jax.experimental import pallas as pl
from jax.experimental.pallas import tpu as pltpu
from jax.sharding import PartitionSpec as P


def slot_table(offsets, request_adapter, page_table, first, rows, used):
    reqs = offsets.shape[0] - 1
    adapter_ids = jnp.arange(page_table.shape[0], dtype=jnp.int32)
    match = (request_adapter[:, None] == adapter_ids[None, :]).astype(jnp.int32)
    page_of_request = jnp.sum(match * page_table[None, :], axis=1)
    leading = jnp.sum((offsets[1:] <= first).astype(jnp.int32))
    wanted = leading + jnp.arange(used, dtype=jnp.int32)
    clipped = jnp.clip(wanted, 0, reqs - 1)
    valid = (wanted < reqs) & (offsets[clipped] < first + rows)
    return (leading, page_of_request[clipped], valid)


def token_select(positions, offsets, leading, used):
    request = jnp.sum((offsets[None, 1:] <= positions[:, None]).astype(jnp.int32), axis=1)
    slot_of = request - leading
    return (slot_of[:, None] == jnp.arange(used, dtype=jnp.int32)[None, :]).astype(jnp.float32)


def shrink_term(local, factors, select):
    scores = jnp.einsum("tf,kfr->tkr", local, factors, preferred_element_type=jnp.float32)
    return jnp.sum(select[:, :, None] * scores, axis=1)


def expand_term(shrunk, factors, select):
    spread = (select[:, :, None] * shrunk[:, None, :].astype(jnp.float32)).astype(jnp.bfloat16)
    return jnp.einsum("tkr,krc->tc", spread, factors, preferred_element_type=jnp.float32)


def body(
    activations, query_weight, offsets, request_adapter, page_table, shrink_pages, expand_pages
):
    rows = activations.shape[0]
    shards = lax.axis_size(("dp", "pipe"))
    reqs = offsets.shape[0] - 1
    shortest = rows * shards // (2 * reqs)
    used = (rows - 2) // shortest + 2
    here = lax.axis_index(("dp", "pipe"))
    first = here * rows
    positions = first + jnp.arange(rows, dtype=jnp.int32)
    leading, pages, valid = slot_table(offsets, request_adapter, page_table, first, rows, used)
    select = token_select(positions, offsets, leading, used)
    whole = lax.all_gather(activations, "tensor", axis=1, tiled=True)
    base = jnp.dot(
        whole,
        lax.all_gather(query_weight, ("dp", "pipe"), axis=0, tiled=True),
        preferred_element_type=jnp.float32,
    )
    shrink_all, expand_all = (
        lax.all_gather(shrink_pages, ("dp", "pipe"), axis=0, tiled=True),
        lax.all_gather(expand_pages, ("dp", "pipe"), axis=0, tiled=True),
    )
    shrink_used = jnp.take(shrink_all, pages, axis=0)
    expand_used = jnp.take(expand_all, pages, axis=0)
    partial_value = shrink_term(activations, shrink_used, select)
    shrunk = lax.psum(partial_value, "tensor").astype(jnp.bfloat16)
    added = expand_term(shrunk, expand_used, select)
    return (base + added).astype(jnp.bfloat16)


MESH = pl.DeviceIdType.MESH
LANES = 128
CHUNKS = 8
HALVES = 2


def relay_kernel(
    act, weight, shrink, expand, slots, out,
    xp, ab, fb, wv, sv, ev, mv, part, rsb, sh, spread, cs, rc, sx, rx, ov,
    load_sem, own_send, own_recv, fwd_send, fwd_recv, xown_send, xown_recv,
    up_send, dn_send, flow_recv, f_send, f_recv, c_send, rs_send, rs_recv, ag_send, ag_recv,
    cs_send, cs_recv, x_send, x_recv, out_sem,
):
    x, p, z = lax.axis_index("dp"), lax.axis_index("pipe"), lax.axis_index("tensor")
    nz = lax.axis_size("tensor")
    rows = act.shape[0]
    ch = rows // CHUNKS
    hf = rows // HALVES
    d = 2 * x + p
    core, other = {"pipe": 1 - p}, {"dp": 1 - x}
    origin = z == d

    def blk(k):
        return 2 * (x if k < 2 else 1 - x) + (p if k % 2 == 0 else 1 - p)

    def rcopy(src, dst, ss, rs, dev):
        return pltpu.make_async_remote_copy(
            src_ref=src, dst_ref=dst, send_sem=ss, recv_sem=rs, device_id=dev, device_id_type=MESH
        )

    def cr(c):
        return pl.ds(c * ch, ch)

    def hr(h):
        return pl.ds(h * hf, hf)

    loads = [
        pltpu.make_async_copy(act, xp.at[d], load_sem.at[0]),
        pltpu.make_async_copy(slots, mv, load_sem.at[2]),
        pltpu.make_async_copy(weight, wv, load_sem.at[3]),
        pltpu.make_async_copy(expand, ev, load_sem.at[4]),
        pltpu.make_async_copy(shrink, sv, load_sem.at[1]),
    ]
    for cp in loads:
        cp.start()
    barrier = pltpu.get_barrier_semaphore()
    for j in range(1, nz):
        pl.semaphore_signal(barrier, inc=1, device_id={"tensor": lax.rem(z + j, nz)}, device_id_type=MESH)
    pl.semaphore_signal(barrier, inc=1, device_id=core, device_id_type=MESH)
    pl.semaphore_signal(barrier, inc=1, device_id=other, device_id_type=MESH)
    pl.semaphore_wait(barrier, nz + 1)
    loads[0].wait()

    def own_x(c):
        s = xp.at[d, cr(c)]
        return rcopy(s, s, xown_send.at[c], xown_recv.at[c], other)

    def own_core(c):
        s = xp.at[d, cr(c)]
        return rcopy(s, s, own_send.at[c], own_recv.at[c], core)

    def fwd(c):
        s = xp.at[blk(2), cr(c)]
        return rcopy(s, s, fwd_send.at[c], fwd_recv.at[c], core)

    def flow(k, c, src, step):
        b = blk(k)
        sem = up_send if step == 1 else dn_send
        return rcopy(
            src.at[b, cr(c)], ab.at[b, cr(c)], sem.at[k, c], flow_recv.at[k, c], {"tensor": z + step}
        )

    up = (z >= d) & (z < nz - 1)
    dn = (z <= d) & (z > 0)

    def goes(k, step):
        if k != 2:
            return up if step == 1 else dn
        return (up & (x == 1)) if step == 1 else (dn & (x == 0))

    def send_flow(k, c, src):
        @pl.when(goes(k, 1))
        def _():
            flow(k, c, src, 1).start()

        @pl.when(goes(k, -1))
        def _():
            flow(k, c, src, -1).start()

    def arrive(k, c):
        s = ab.at[blk(k), cr(c)]
        rcopy(s, s, up_send.at[k, c], flow_recv.at[k, c], core).wait_recv()

    def relay(k, c):
        @pl.when(jnp.logical_not(origin))
        def _():
            arrive(k, c)
            send_flow(k, c, ab)

    dx = blk(2)
    f_origin = z == dx
    f_member = ((x == 1) & (z > dx)) | ((x == 0) & (z < dx))
    f_next = (f_origin | f_member) & (((x == 1) & (z < nz - 1)) | ((x == 0) & (z > 0)))

    def f_copy(c, src):
        return rcopy(src, fb.at[cr(c)], f_send.at[c], f_recv.at[c], {"tensor": z + 2 * x - 1})

    def cross(c):
        return rcopy(fb.at[cr(c)], ab.at[d, cr(c)], c_send.at[c], flow_recv.at[2, c], other)

    def f_relay(c):
        @pl.when(f_member)
        def _():
            s = fb.at[cr(c)]
            rcopy(s, s, f_send.at[c], f_recv.at[c], core).wait_recv()

            @pl.when(f_next)
            def _():
                f_copy(c, fb.at[cr(c)]).start()

            cross(c).start()

    for c in range(CHUNKS):
        own_x(c).start()
        own_core(c).start()

        @pl.when(f_origin & f_next)
        def _():
            f_copy(c, xp.at[d, cr(c)]).start()

        @pl.when(origin)
        def _():
            send_flow(0, c, xp)

    groups = shrink.shape[0] * shrink.shape[1] // LANES
    half = LANES // 2

    def shrink_block(k):
        b = blk(k)
        folded = []
        for h in range(HALVES):
            m = mv[b, hr(h), :]

            def add(q, total):
                pair = sv[pl.ds(4 * q, 4)].reshape(2 * LANES, sv.shape[2])
                scores = lax.dot_general(
                    xp[b, hr(h), :], pair, (((1,), (1,)), ((), ())), preferred_element_type=jnp.float32
                )
                total += jnp.where(m == 4 * q, scores[:, :LANES], 0.0)
                return total + jnp.where(m == 4 * q + 2, scores[:, LANES:], 0.0)

            total = lax.fori_loop(0, groups // 2, add, jnp.zeros((hf, LANES), jnp.float32))
            folded.append(total[:, :half] + total[:, half:])
        part[b] = jnp.concatenate(folded, axis=1).astype(jnp.bfloat16)

    steps = CHUNKS // 2
    for i in range(steps):
        for c in (2 * i, 2 * i + 1):
            own_x(c).wait_recv()
            fwd(c).start()

            @pl.when(origin)
            def _():
                send_flow(2, c, xp)

        if i == 0:
            loads[1].wait()
            loads[4].wait()
            shrink_block(0)
        if i == 1:
            for c in range(CHUNKS):
                own_core(c).wait_recv()
            shrink_block(1)
        if i > 0:
            for c in (2 * i - 2, 2 * i - 1):
                relay(0, c)
                f_relay(c)
    for c in range(CHUNKS):
        fwd(c).wait_recv()

        @pl.when(origin)
        def _():
            send_flow(3, c, xp)

    @pl.when(origin)
    def _():
        for c in range(CHUNKS):
            send_flow(1, c, xp)

    shrink_block(2)
    for c in (CHUNKS - 2, CHUNKS - 1):
        relay(0, c)
        f_relay(c)
    shrink_block(3)

    def rs_copy(j):
        to = lax.rem(z + j, nz)
        return rcopy(part.at[to], rsb.at[j - 1], rs_send.at[j - 1], rs_recv.at[j - 1], {"tensor": to})

    def ag_copy(j):
        to = lax.rem(z + j, nz)
        return rcopy(sh.at[z], sh.at[z], ag_send.at[j - 1], ag_recv.at[j - 1], {"tensor": to})

    for j in range(1, nz):
        rs_copy(j).start()
    relay(3, 0)
    relay(3, 1)
    for j in range(1, nz):
        rs_copy(j).wait_recv()
    total = part[z].astype(jnp.float32)
    for j in range(1, nz):
        total += rsb[j - 1].astype(jnp.float32)
    sh[z] = total.astype(jnp.bfloat16)
    for j in range(1, nz):
        ag_copy(j).start()
    relay(3, 2)
    relay(3, 3)
    for j in range(1, nz):
        ag_copy(j).wait_recv()
    loads[2].wait()
    loads[3].wait()

    @pl.when(origin)
    def _():
        cp = pltpu.make_async_copy(xp, ab, load_sem.at[5])
        cp.start()
        cp.wait()

    tile = min(512, wv.shape[1])

    def compute(k, h, emit):
        b = blk(k)
        m = mv[b, hr(h), :]
        s = sh[b][:, h * half:(h + 1) * half]
        s = jnp.concatenate([s, s], axis=1)
        for g in range(groups):
            spread[:, g * LANES:(g + 1) * LANES] = jnp.where(m == 2 * g, s, jnp.zeros_like(s))

        def step(n, _):
            cols = pl.ds(pl.multiple_of(n * tile, tile), tile)
            value = jnp.dot(ab[b, hr(h), :], wv[:, cols], preferred_element_type=jnp.float32)
            value += jnp.dot(spread[...], ev[:, :, cols].reshape(spread.shape[1], tile), preferred_element_type=jnp.float32)
            emit(value, cols)
            return 0

        lax.fori_loop(0, wv.shape[1] // tile, step, 0)

    def core_copy(i, h):
        return rcopy(cs.at[i, hr(h)], rc.at[i, hr(h)], cs_send.at[i, h], cs_recv.at[i, h], core)

    def x_copy(h):
        return rcopy(sx.at[hr(h)], rx.at[hr(h)], x_send.at[h], x_recv.at[h], other)

    def out_copy(h):
        return pltpu.make_async_copy(ov.at[hr(h)], out.at[hr(h)], out_sem.at[h])

    def to_core(i, k, h):
        def emit(value, cols):
            cs[i, hr(h), cols] = value.astype(jnp.bfloat16)

        compute(k, h, emit)
        core_copy(i, h).start()

    def to_x(h):
        core_copy(1, h).wait_recv()

        def emit(value, cols):
            sx[hr(h), cols] = (value + rc[1, hr(h), cols].astype(jnp.float32)).astype(jnp.bfloat16)

        compute(2, h, emit)
        x_copy(h).start()

    per = CHUNKS // HALVES

    def arrive_half(h):
        @pl.when(jnp.logical_not(origin))
        def _():
            for c in range(per * h, per * (h + 1)):
                arrive(2, c)

    def final(h):
        core_copy(0, h).wait_recv()
        x_copy(h).wait_recv()

        def emit(value, cols):
            value += rc[0, hr(h), cols].astype(jnp.float32) + rx[hr(h), cols].astype(jnp.float32)
            ov[hr(h), cols] = value.astype(jnp.bfloat16)

        compute(0, h, emit)
        out_copy(h).start()

    def relay_pair(k, i):
        relay(k, 2 * i)
        relay(k, 2 * i + 1)

    to_core(1, 3, 0)
    relay_pair(3, 2)
    arrive_half(0)
    to_x(0)
    relay_pair(3, 3)
    to_core(1, 3, 1)
    relay_pair(1, 0)
    arrive_half(1)
    to_x(1)
    relay_pair(1, 1)
    to_core(0, 1, 0)
    relay_pair(1, 2)
    final(0)
    relay_pair(1, 3)
    to_core(0, 1, 1)
    final(1)

    for h in range(HALVES):
        out_copy(h).wait()
        core_copy(0, h).wait_send()
        core_copy(1, h).wait_send()
        x_copy(h).wait_send()
    for j in range(1, nz):
        rs_copy(j).wait_send()
        ag_copy(j).wait_send()
    for c in range(CHUNKS):
        own_x(c).wait_send()
        own_core(c).wait_send()
        fwd(c).wait_send()
    for c in range(CHUNKS):
        for k in range(4):

            @pl.when(goes(k, 1))
            def _():
                flow(k, c, ab, 1).wait_send()

            @pl.when(goes(k, -1))
            def _():
                flow(k, c, ab, -1).wait_send()

        @pl.when(f_next)
        def _():
            f_copy(c, fb.at[cr(c)]).wait_send()

        @pl.when(f_member)
        def _():
            cross(c).wait_send()


def relay_body(
    activations, query_weight, offsets, request_adapter, page_table, shrink_pages, expand_pages
):
    rows, feats = activations.shape
    cols = query_weight.shape[1]
    shards = lax.axis_size(("dp", "pipe"))
    held, _, rank = shrink_pages.shape
    shard = lax.axis_index(("dp", "pipe"))
    adapter_ids = jnp.arange(page_table.shape[0], dtype=jnp.int32)
    match = (request_adapter[:, None] == adapter_ids[None, :]).astype(jnp.int32)
    page_of_request = jnp.sum(match * page_table[None, :], axis=1)
    positions = jnp.arange(rows * shards, dtype=jnp.int32)
    inside = (offsets[None, :-1] <= positions[:, None]) & (positions[:, None] < offsets[None, 1:])
    slot = jnp.sum(jnp.where(inside, page_of_request[None, :], 0), axis=1) - shard * held
    slot = jnp.where((slot >= 0) & (slot < held), slot, -8)
    upper = (jnp.arange(LANES, dtype=jnp.int32) >= rank).astype(jnp.int32)
    slots = (slot[:, None] - upper[None, :]).reshape(shards, rows, LANES)
    bf, dma = jnp.bfloat16, pltpu.SemaphoreType.DMA
    hf = rows // HALVES
    nz = lax.axis_size("tensor")
    return pl.pallas_call(
        relay_kernel,
        out_shape=jax.ShapeDtypeStruct((rows, cols), bf),
        in_specs=[pl.BlockSpec(memory_space=pl.ANY)] * 5,
        out_specs=pl.BlockSpec(memory_space=pl.ANY),
        scratch_shapes=[
            pltpu.VMEM((shards, rows, feats), bf),
            pltpu.VMEM((shards, rows, feats), bf),
            pltpu.VMEM((rows, feats), bf),
            pltpu.VMEM(query_weight.shape, bf),
            pltpu.VMEM((held, rank, feats), bf),
            pltpu.VMEM(expand_pages.shape, bf),
            pltpu.VMEM(slots.shape, jnp.int32),
            pltpu.VMEM((shards, rows // 2, LANES), bf),
            pltpu.VMEM((nz - 1, rows // 2, LANES), bf),
            pltpu.VMEM((shards, rows // 2, LANES), bf),
            pltpu.VMEM((hf, held * rank), bf),
            pltpu.VMEM((2, rows, cols), bf),
            pltpu.VMEM((2, rows, cols), bf),
            pltpu.VMEM((rows, cols), bf),
            pltpu.VMEM((rows, cols), bf),
            pltpu.VMEM((rows, cols), bf),
            dma((6,)),
            dma((CHUNKS,)), dma((CHUNKS,)), dma((CHUNKS,)), dma((CHUNKS,)), dma((CHUNKS,)), dma((CHUNKS,)),
            dma((4, CHUNKS)), dma((4, CHUNKS)), dma((4, CHUNKS)),
            dma((CHUNKS,)), dma((CHUNKS,)), dma((CHUNKS,)),
            dma((nz - 1,)), dma((nz - 1,)), dma((nz - 1,)), dma((nz - 1,)),
            dma((2, HALVES)), dma((2, HALVES)), dma((HALVES,)), dma((HALVES,)), dma((HALVES,)),
        ],
        compiler_params=pltpu.CompilerParams(
            collective_id=0, has_side_effects=True, vmem_limit_bytes=62 * 1024 * 1024
        ),
        cost_estimate=pl.CostEstimate(
            flops=2 * shards * rows * feats * cols, bytes_accessed=2 * feats * cols, transcendentals=0
        ),
    )(activations, query_weight, shrink_pages.transpose(0, 2, 1), expand_pages, slots)


def solution(mesh):
    small = mesh.shape["dp"] == 2 and mesh.shape["pipe"] == 2 and mesh.shape["tensor"] == 4
    return jax.shard_map(
        relay_body if small else body,
        mesh=mesh,
        in_specs=(
            P(("groups", "dp", "pipe"), "tensor"),
            P(("dp", "pipe"), "tensor"),
            P("groups"),
            P("groups"),
            P("groups"),
            P(("groups", "dp", "pipe"), "tensor", None),
            P(("groups", "dp", "pipe"), None, "tensor"),
        ),
        out_specs=P(("groups", "dp", "pipe"), "tensor"),
        check_vma=False,
    )
```
